32 devices in a mesh: frames: 2 (over x), date: 16 (over z, y, core).
Axes of the slice: x: 2, y: 2, z: 4, core: 2. Of those that a mesh axis runs over, the one named last changes fastest.
Arguments:
- slc: float32 [2, 256, 288, 48], P(None, 'date', 'frames'), parts along dimension 2, may hold values from -6 to 6
Outputs:
- coherence: bfloat16 [96, 8, 256, 256], P(('frames', 'date')), parts along dimension 0
The draws below stay inside these ranges and needn't reach their ends.
There are 2 independent parts, one for each index of `frames`. The reference program is written for one: setup_inputs(seed, part) draws one part's arguments, and reference() takes and returns one part's arrays. A program takes and returns all parts, laid end to end along the dimension named above; each array names one. Nothing has to cross between parts.
All inputs are finite; a program needn't handle non-finite values.
Results may differ from the reference program's by a relative error of at most 0.001.
Values sent between devices are 32-bit elements; how exact they have to be, the bound alone decides.
A program may use at most 128 MiB of HBM per device.

```python
import jax
import jax.numpy as jnp
from jax import lax

DATES = 256
BOX_AZ = 11
BOX_RG = 23
STEP_AZ = 3
STEP_RG = 6
MARGIN = 8
OA = 48
AZ = 144
RG = 48


def levels(key, shape, pieces, low, largest):
    factor_of = 1.0
    for axis_at, shards_of in pieces:
        draws = jax.random.uniform(jax.random.fold_in(jax.random.fold_in(key, 6), axis_at), (shards_of,), jnp.float32, low / len(pieces), largest / len(pieces))
        factor_of = factor_of * jnp.repeat(jnp.exp(draws), shape[axis_at] // shards_of).reshape((-1,) + (1,) * (len(shape) - 1 - axis_at))
    return factor_of


def bell_draw(own_key, extent, scale, reach, split=(), kind=jnp.bfloat16):
    array = jax.random.normal(own_key, extent, jnp.float32) * scale
    if len(split) > 0:
        array = levels(own_key, extent, split, -0.22, 0.18) * array
    return jnp.clip(array, min=-reach, max=reach).astype(kind)


def setup_inputs(seed: int = 0, part: int = 0) -> dict:
    seeds = jax.random.split(jax.random.key(seed), 2)
    part_splits = jax.random.split(jax.random.fold_in(seeds[1], part), 2)
    return {
        "slc": bell_draw(part_splits[0], (2, DATES, AZ, RG), 1.0, 6.0, ((1, 16),), jnp.float32),
    }


def coherence_rows(with_margin, out_rows):
    date_count = with_margin.shape[1]
    range_width = with_margin.shape[3]
    range_cols = range_width // STEP_RG
    stacked = with_margin.reshape(2 * date_count, with_margin.shape[2] * range_width)
    span = BOX_AZ * range_width
    column = lax.broadcasted_iota(jnp.int32, (range_cols, span), 1) % range_width
    first = lax.broadcasted_iota(jnp.int32, (range_cols, span), 0) * STEP_RG
    inside = ((column >= first) & (column < first + BOX_RG)).astype(stacked.dtype)
    lower = lax.broadcasted_iota(jnp.int32, (date_count, date_count), 0)
    upper = lax.broadcasted_iota(jnp.int32, (date_count, date_count), 1)

    def one_row(row_index):
        start = (row_index * (STEP_AZ * range_width)).astype(jnp.int32)
        window = lax.dynamic_slice_in_dim(stacked, start, span, 1)
        masked = inside[:, None, :] * window[None]
        gram = jnp.einsum('rak,bk->rab', masked, window, precision=lax.Precision.HIGHEST)
        real_part = gram[:, :date_count, :date_count] + gram[:, date_count:, date_count:]
        imag_part = gram[:, date_count:, :date_count] - gram[:, :date_count, date_count:]
        powers = jnp.diagonal(real_part, axis1=1, axis2=2)
        inverse = 1.0 / jnp.sqrt(powers)
        scale = inverse[:, :, None] * inverse[:, None, :]
        packed = jnp.where((upper >= lower)[None], real_part * scale, imag_part * scale)
        return packed.astype(jnp.bfloat16)
    return lax.map(one_row, jnp.arange(out_rows, dtype=jnp.int32))

def reference(slc):
    zero_rows = jnp.zeros((2, slc.shape[1], MARGIN, slc.shape[3]), slc.dtype)
    with_margin = jnp.concatenate([slc, zero_rows], axis=2)
    return coherence_rows(with_margin, OA)
```

```python
import functools

import jax
import jax.numpy as jnp
from jax import lax
from jax.experimental import pallas as pl
from jax.experimental.pallas import tpu as pltpu
from jax.sharding import PartitionSpec as P

BOX_AZ = 11
BOX_RG = 23
STEP_AZ = 3
STEP_RG = 6
MARGIN = 8
LANES = 128
MESH = pl.DeviceIdType.MESH


def round_up(value, multiple):
    return -(-value // multiple) * multiple


def exchange_kernel(axis, count, margin_lanes, x_ref, slab_ref, below_ref, send_sem, recv_sem, fsend_sem, frecv_sem, own_sem):
    me = lax.axis_index(axis)
    before = lax.rem(me + count - 1, count)
    barrier = pltpu.get_barrier_semaphore()

    def greet(step, carry):
        pl.semaphore_signal(barrier, inc=1, device_id={axis: lax.rem(me + step, count)}, device_id_type=MESH)
        return carry

    lax.fori_loop(1, count, greet, 0)
    pl.semaphore_wait(barrier, count - 1)

    def slab_copy(step):
        to = lax.rem(me + step, count)
        return pltpu.make_async_remote_copy(
            src_ref=x_ref.at[to],
            dst_ref=slab_ref.at[:, me],
            send_sem=send_sem.at[step],
            recv_sem=recv_sem.at[step],
            device_id={axis: to},
            device_id_type=MESH,
        )

    def slab_arrival(step):
        source = lax.rem(me + count - step, count)
        return pltpu.make_async_remote_copy(
            src_ref=x_ref.at[source],
            dst_ref=slab_ref.at[:, source],
            send_sem=send_sem.at[step],
            recv_sem=recv_sem.at[step],
            device_id={axis: source},
            device_id_type=MESH,
        )

    def below_copy(step):
        source = lax.rem(me + count - step, count)
        return pltpu.make_async_remote_copy(
            src_ref=slab_ref.at[:, source, :, 0:margin_lanes],
            dst_ref=below_ref.at[:, source],
            send_sem=fsend_sem.at[source],
            recv_sem=frecv_sem.at[source],
            device_id={axis: before},
            device_id_type=MESH,
        )

    def start(step, carry):
        slab_copy(step).start()
        return carry

    lax.fori_loop(1, count, start, 0)
    own = pltpu.make_async_copy(x_ref.at[me], slab_ref.at[:, me], own_sem)
    own.start()
    own.wait()

    @pl.when(me > 0)
    def _():
        below_copy(0).start()

    def arrive(step, carry):
        slab_arrival(step).wait_recv()

        @pl.when(me > 0)
        def _():
            below_copy(step).start()

        return carry

    lax.fori_loop(1, count, arrive, 0)

    def finish(step, carry):
        @pl.when(step > 0)
        def _():
            slab_copy(step).wait_send()

        @pl.when(me > 0)
        def _():
            below_copy(step).wait_send()

        @pl.when(me < count - 1)
        def _():
            below_copy(step).wait_recv()

        return carry

    lax.fori_loop(0, count, finish, 0)


def exchange(messages, axis, margin_lanes):
    count, parts, dates, lanes = messages.shape
    return pl.pallas_call(
        functools.partial(exchange_kernel, axis, count, margin_lanes),
        out_shape=(
            jax.ShapeDtypeStruct((parts, count, dates, lanes), jnp.float32),
            jax.ShapeDtypeStruct((parts, count, dates, margin_lanes), jnp.float32),
        ),
        in_specs=[pl.BlockSpec(memory_space=pl.ANY)],
        out_specs=(pl.BlockSpec(memory_space=pl.ANY), pl.BlockSpec(memory_space=pl.ANY)),
        scratch_shapes=[pltpu.SemaphoreType.DMA((count,))] * 4 + [pltpu.SemaphoreType.DMA],
        compiler_params=pltpu.CompilerParams(collective_id=0, has_side_effects=True),
    )(messages)


def gram_kernel(axis, dates, range_width, slab_lanes, slab_ref, below_ref, pick_ref, out_ref, high, low, partial):
    groups = range_width // STEP_RG
    out_row = pl.program_id(0)

    @pl.when(out_row == 0)
    def _():
        not_last = lax.axis_index(axis) < lax.axis_size(axis) - 1
        below = jnp.where(not_last, below_ref[...], 0.0)
        for at, value in ((0, slab_ref[...]), (slab_lanes, below)):
            big = value.astype(jnp.bfloat16)
            small = (value - big.astype(jnp.float32)).astype(jnp.bfloat16)
            pick = pick_ref[at:at + value.shape[1], :]
            for half, held in ((big, high), (small, low)):
                moved = jnp.dot(half, pick, preferred_element_type=jnp.float32)
                if at == 0:
                    held[...] = moved.astype(jnp.bfloat16)
                else:
                    held[...] = held[...] + moved.astype(jnp.bfloat16)

    lane = lax.broadcasted_iota(jnp.int32, (1, LANES), 1)
    row, column = lane // STEP_RG, lane % STEP_RG
    first = out_row * STEP_AZ
    in_rows = (row >= first) & (row < first + BOX_AZ)
    lower = lax.broadcasted_iota(jnp.int32, (dates, dates), 0)
    upper = lax.broadcasted_iota(jnp.int32, (dates, dates), 1)
    real_side = upper >= lower
    reach = (BOX_RG - 1) // STEP_RG
    short = BOX_RG - reach * STEP_RG

    def packed(group, inside):
        at = pl.ds(group * LANES, LANES)
        rh, rl = high[0:dates, at], low[0:dates, at]
        ih, il = high[dates:, at], low[dates:, at]
        keep = jnp.where(inside, 1.0, 0.0).astype(jnp.bfloat16)
        rhm, rlm, ihm, ilm = rh * keep, rl * keep, ih * keep, il * keep
        right = jnp.concatenate([rh, rl, rh, ih, il, ih], axis=1)
        left_re = jnp.concatenate([rhm, rhm, rlm, ihm, ihm, ilm], axis=1)
        left_im = jnp.concatenate([ihm, ihm, ilm, -rhm, -rhm, -rlm], axis=1)
        dims = (((1,), (1,)), ((), ()))
        real = lax.dot_general(left_re, right, dims, preferred_element_type=jnp.float32)
        imag = lax.dot_general(left_im, right, dims, preferred_element_type=jnp.float32)
        return jnp.where(real_side, real, imag)

    for group in range(groups):
        if group >= reach:
            total = packed(group, in_rows & (column < short))
            write(out_ref, group - reach, [partial[g] for g in range(group - reach, group)] + [total], lower == upper)
            partial[group] = total + packed(group, in_rows & (column >= short))
        else:
            partial[group] = packed(group, in_rows)
    for group in range(max(0, groups - reach), groups):
        write(out_ref, group, [partial[g] for g in range(group, groups)], lower == upper)


def write(out_ref, column, terms, diagonal):
    total = terms[0]
    for term in terms[1:]:
        total = total + term
    power = jnp.where(diagonal, total, 0.0)
    down = 1.0 / jnp.sqrt(jnp.sum(power, axis=1, keepdims=True))
    across = 1.0 / jnp.sqrt(jnp.sum(power, axis=0, keepdims=True))
    out_ref[0, column] = (total * (down * across)).astype(out_ref.dtype)


def coherence_rows(slab, below, axis, out_rows, slab_height, range_width):
    dates = slab.shape[0] // 2
    groups = range_width // STEP_RG
    slab_lanes, margin_lanes = slab.shape[1], below.shape[1]
    source = jnp.arange(slab_lanes + margin_lanes)[:, None]
    target = jnp.arange(groups * LANES)[None]
    group, within = target // LANES, target % LANES
    row, column = within // STEP_RG, group * STEP_RG + within % STEP_RG
    wanted = jnp.where(
        row < slab_height,
        row * range_width + column,
        slab_lanes + (row - slab_height) * range_width + column,
    )
    wanted = jnp.where(row < slab_height + MARGIN, wanted, -1)
    pick = (source == wanted).astype(jnp.bfloat16)
    return pl.pallas_call(
        functools.partial(gram_kernel, axis, dates, range_width, slab_lanes),
        grid=(out_rows,),
        out_shape=jax.ShapeDtypeStruct((out_rows, groups, dates, dates), jnp.bfloat16),
        in_specs=[
            pl.BlockSpec(slab.shape, lambda a: (0, 0)),
            pl.BlockSpec(below.shape, lambda a: (0, 0)),
            pl.BlockSpec(pick.shape, lambda a: (0, 0)),
        ],
        out_specs=pl.BlockSpec((1, groups, dates, dates), lambda a: (a, 0, 0, 0)),
        scratch_shapes=[
            pltpu.VMEM((2 * dates, groups * LANES), jnp.bfloat16),
            pltpu.VMEM((2 * dates, groups * LANES), jnp.bfloat16),
            pltpu.VMEM((groups, dates, dates), jnp.float32),
        ],
        compiler_params=pltpu.CompilerParams(vmem_limit_bytes=48 * 1024 * 1024),
    )(slab, below, pick)


def on_device(slc):
    axis = "date"
    count = lax.axis_size(axis)
    parts, dates, height, width = slc.shape
    slab_height = height // count
    slab = slab_height * width
    messages = slc.reshape(parts, dates, count, slab).transpose(2, 0, 1, 3)
    messages = jnp.pad(messages, ((0, 0),) * 3 + ((0, round_up(slab, LANES) - slab),))
    slabs, below = exchange(messages, axis, MARGIN * width)
    slabs = slabs.reshape(parts * count * dates, -1)
    below = below.reshape(parts * count * dates, -1)
    return coherence_rows(slabs, below, axis, slab_height // STEP_AZ, slab_height, width)


def solution(mesh):
    in_specs = (P(None, "date", "frames", None),)
    out_specs = P(("frames", "date"), None, None, None)
    return jax.shard_map(
        on_device, mesh=mesh, in_specs=in_specs, out_specs=out_specs, check_vma=False
    )
```

```python
import functools

import jax
import jax.numpy as jnp
from jax import lax
from jax.experimental import pallas as pl
from jax.experimental.pallas import tpu as pltpu
from jax.sharding import PartitionSpec as P

BOX_AZ = 11
BOX_RG = 23
STEP_AZ = 3
STEP_RG = 6
MARGIN = 8
LANES = 128
PARTS = 2
MESH = pl.DeviceIdType.MESH
CONTRACT_LANES = (((1,), (1,)), ((), ()))


def round_up(value, multiple):
    return -(-value // multiple) * multiple


def split_in_two(value):
    big = value.astype(jnp.bfloat16)
    return big, (value - big.astype(jnp.float32)).astype(jnp.bfloat16)


def fill_pick(pick, blocks, tail, slab_height, width):
    target = lax.broadcasted_iota(jnp.int32, (1, pick.shape[1]), 1)
    within = target % LANES
    row, column = within // STEP_RG, target // LANES * STEP_RG + within % STEP_RG
    main = blocks * LANES
    wanted = jnp.where(row < MARGIN, row * width + column, main + (row - MARGIN) * width + column)
    below = main + PARTS * tail * LANES
    wanted = jnp.where(row >= slab_height, below + (row - slab_height) * width + column, wanted)
    wanted = jnp.where(row < slab_height + MARGIN, wanted, -1)
    in_tail = (row >= MARGIN) & (row < slab_height)
    tail_width = (slab_height - MARGIN) * width
    other = jnp.where(in_tail, wanted + tail * LANES + tail_width, -1)
    for at in range(0, pick.shape[0], LANES):
        source = at + lax.broadcasted_iota(jnp.int32, (LANES, pick.shape[1]), 0)
        taken = (source == wanted) | (source == other)
        pick[at:at + LANES, :] = jnp.where(taken, 1.0, 0.0).astype(jnp.bfloat16)


def kernel(axis, slab_height, width, x_ref, out_ref, slab, below, pick, high, low, partial, rows_out,
           send_sem, recv_sem, fsend_sem, frecv_sem, own_sem, out_sem):
    count, dates = slab.shape[1], slab.shape[1] * slab.shape[2]
    blocks = below.shape[0] // PARTS
    groups = width // STEP_RG
    out_rows = slab_height // STEP_AZ
    me = lax.axis_index(axis)
    before = lax.rem(me + count - 1, count)
    barrier = pltpu.get_barrier_semaphore()

    def greet(step, carry):
        pl.semaphore_signal(barrier, inc=1, device_id={axis: lax.rem(me + step, count)}, device_id_type=MESH)
        return carry

    lax.fori_loop(1, count, greet, 0)
    pl.semaphore_wait(barrier, count - 1)

    def slab_copy(step, to, source):
        return pltpu.make_async_remote_copy(
            src_ref=x_ref.at[to],
            dst_ref=slab.at[:, source],
            send_sem=send_sem.at[step],
            recv_sem=recv_sem.at[step],
            device_id={axis: to},
            device_id_type=MESH,
        )

    def below_copy(block):
        return pltpu.make_async_remote_copy(
            src_ref=slab.at[pl.ds(PARTS * block, PARTS)],
            dst_ref=below.at[pl.ds(PARTS * block, PARTS)],
            send_sem=fsend_sem.at[block],
            recv_sem=frecv_sem.at[block],
            device_id={axis: before},
            device_id_type=MESH,
        )

    def start(step, carry):
        slab_copy(step, lax.rem(me + step, count), me).start()
        return carry

    lax.fori_loop(1, count, start, 0)
    own = pltpu.make_async_copy(x_ref.at[me], slab.at[:, me], own_sem)
    own.start()
    fill_pick(pick, blocks, 1, slab_height, width)
    own.wait()

    def arrive(step, carry):
        source = lax.rem(me + count - step, count)
        slab_copy(step, source, source).wait_recv()
        return carry

    lax.fori_loop(1, count, arrive, 0)

    @pl.when(me > 0)
    def _():
        for block in range(blocks):
            below_copy(block).start()

    for part in range(PARTS):
        tiles = [PARTS * block + part for block in range(blocks)] + [PARTS * blocks]
        value = jnp.concatenate([slab[t].reshape(dates, LANES) for t in tiles], axis=1)
        main = blocks * LANES
        mine = jnp.concatenate([pick[0:main, :], pick[main + part * LANES:main + (part + 1) * LANES, :]], axis=0)
        for half, held in zip(split_in_two(value), (high, low)):
            moved = jnp.dot(half, mine, preferred_element_type=jnp.float32)
            held[part * dates:(part + 1) * dates, :] = moved.astype(jnp.bfloat16)

    lane = lax.broadcasted_iota(jnp.int32, (1, LANES), 1)
    row, column = lane // STEP_RG, lane % STEP_RG
    lower = lax.broadcasted_iota(jnp.int32, (dates, dates), 0)
    upper = lax.broadcasted_iota(jnp.int32, (dates, dates), 1)
    reach = (BOX_RG - 1) // STEP_RG
    short = BOX_RG - reach * STEP_RG

    def packed(group, inside):
        at = slice(group * LANES, (group + 1) * LANES)
        rh, rl = high[0:dates, at], low[0:dates, at]
        ih, il = high[dates:, at], low[dates:, at]
        keep = jnp.where(inside, 1.0, 0.0).astype(jnp.bfloat16)
        rhm, rlm, ihm, ilm = rh * keep, rl * keep, ih * keep, il * keep
        right = jnp.concatenate([rh, rl, rh, ih, il, ih], axis=1)
        left_re = jnp.concatenate([rhm, rhm, rlm, ihm, ihm, ilm], axis=1)
        left_im = jnp.concatenate([ihm, ihm, ilm, -rhm, -rhm, -rlm], axis=1)
        real = lax.dot_general(left_re, right, CONTRACT_LANES, preferred_element_type=jnp.float32)
        imag = lax.dot_general(left_im, right, CONTRACT_LANES, preferred_element_type=jnp.float32)
        return jnp.where(upper >= lower, real, imag)

    def out_copy(out_row, at):
        return pltpu.make_async_copy(rows_out.at[out_row, at], out_ref.at[out_row, at], out_sem.at[out_row, at])

    def write(out_row, at, terms):
        total = terms[0]
        for term in terms[1:]:
            total = total + term
        power = jnp.where(upper == lower, total, 0.0)
        down = 1.0 / jnp.sqrt(jnp.sum(power, axis=1, keepdims=True))
        across = 1.0 / jnp.sqrt(jnp.sum(power, axis=0, keepdims=True))
        rows_out[out_row, at] = (total * (down * across)).astype(rows_out.dtype)
        out_copy(out_row, at).start()

    def one_row(out_row, carry):
        @pl.when(me < count - 1)
        def _():
            below_copy(out_row).wait_recv()
            at = (blocks + PARTS) * LANES + out_row * LANES
            mine = pick[pl.ds(pl.multiple_of(at, LANES), LANES), :]
            for part in range(PARTS):
                value = below[PARTS * out_row + part].reshape(dates, LANES)
                for half, held in zip(split_in_two(value), (high, low)):
                    moved = jnp.dot(half, mine, preferred_element_type=jnp.float32)
                    here = slice(part * dates, (part + 1) * dates)
                    held[here, :] = held[here, :] + moved.astype(jnp.bfloat16)

        first = out_row * STEP_AZ
        in_rows = (row >= first) & (row < first + BOX_AZ)
        for group in range(groups):
            if group >= reach:
                total = packed(group, in_rows & (column < short))
                write(out_row, group - reach, [partial[g] for g in range(group - reach, group)] + [total])
                partial[group] = total + packed(group, in_rows & (column >= short))
            else:
                partial[group] = packed(group, in_rows)
        for group in range(max(0, groups - reach), groups):
            write(out_row, group, [partial[g] for g in range(group, groups)])
        return carry

    lax.fori_loop(0, out_rows, one_row, 0)

    def sent(step, carry):
        slab_copy(step, lax.rem(me + step, count), me).wait_send()
        return carry

    lax.fori_loop(1, count, sent, 0)

    @pl.when(me > 0)
    def _():
        for block in range(blocks):
            below_copy(block).wait_send()

    def written(out_row, carry):
        for at in range(groups):
            out_copy(out_row, at).wait()
        return carry

    lax.fori_loop(0, out_rows, written, 0)


def on_device(slc):
    axis = "date"
    count = lax.axis_size(axis)
    parts, own_dates, height, width = slc.shape
    slab_height = height // count
    out_rows = slab_height // STEP_AZ
    main, tail = MARGIN * width, (slab_height - MARGIN) * width
    blocks = main // LANES
    groups = width // STEP_RG
    dates = count * own_dates
    assert main % LANES == 0 and parts * tail <= LANES and blocks == out_rows
    slabs = slc.reshape(parts, own_dates, count, slab_height * width)
    first = slabs[..., :main].reshape(parts, own_dates, count, blocks, LANES)
    first = first.transpose(2, 3, 0, 1, 4).reshape(count, blocks * parts, own_dates, LANES)
    last = slabs[..., main:].transpose(2, 1, 0, 3).reshape(count, 1, own_dates, parts * tail)
    last = jnp.pad(last, ((0, 0),) * 3 + ((0, LANES - parts * tail),))
    messages = jnp.concatenate([first, last], axis=1)
    wide = groups * LANES
    return pl.pallas_call(
        functools.partial(kernel, axis, slab_height, width),
        out_shape=jax.ShapeDtypeStruct((out_rows, groups, dates, dates), jnp.bfloat16),
        in_specs=[pl.BlockSpec(memory_space=pltpu.VMEM)],
        out_specs=pl.BlockSpec(memory_space=pl.ANY),
        scratch_shapes=[
            pltpu.VMEM((parts * blocks + 1, count, own_dates, LANES), jnp.float32),
            pltpu.VMEM((parts * blocks, count, own_dates, LANES), jnp.float32),
            pltpu.VMEM(((2 * blocks + parts) * LANES, wide), jnp.bfloat16),
            pltpu.VMEM((parts * dates, wide), jnp.bfloat16),
            pltpu.VMEM((parts * dates, wide), jnp.bfloat16),
            pltpu.VMEM((groups, dates, dates), jnp.float32),
            pltpu.VMEM((out_rows, groups, dates, dates), jnp.bfloat16),
            pltpu.SemaphoreType.DMA((count,)),
            pltpu.SemaphoreType.DMA((count,)),
            pltpu.SemaphoreType.DMA((blocks,)),
            pltpu.SemaphoreType.DMA((blocks,)),
            pltpu.SemaphoreType.DMA,
            pltpu.SemaphoreType.DMA((out_rows, groups)),
        ],
        compiler_params=pltpu.CompilerParams(
            collective_id=0, has_side_effects=True, vmem_limit_bytes=48 * 1024 * 1024
        ),
    )(messages)


def solution(mesh):
    in_specs = (P(None, "date", "frames", None),)
    out_specs = P(("frames", "date"), None, None, None)
    return jax.shard_map(
        on_device, mesh=mesh, in_specs=in_specs, out_specs=out_specs, check_vma=False
    )
```

```python
import functools

import jax
import jax.numpy as jnp
from jax import lax
from jax.experimental import pallas as pl
from jax.experimental.pallas import tpu as pltpu
from jax.sharding import PartitionSpec as P

BOX_AZ = 11
BOX_RG = 23
STEP_AZ = 3
STEP_RG = 6
MARGIN = 8
LANES = 128
PARTS = 2
MESH = pl.DeviceIdType.MESH
CONTRACT_LANES = (((1,), (1,)), ((), ()))


def round_up(value, multiple):
    return -(-value // multiple) * multiple


def split_in_two(value):
    big = value.astype(jnp.bfloat16)
    return big, (value - big.astype(jnp.float32)).astype(jnp.bfloat16)


def fill_pick(pick, blocks, tail, slab_height, width):
    target = lax.broadcasted_iota(jnp.int32, (1, pick.shape[1]), 1)
    within = target % LANES
    row, column = within // STEP_RG, target // LANES * STEP_RG + within % STEP_RG
    main = blocks * LANES
    wanted = jnp.where(row < MARGIN, row * width + column, main + (row - MARGIN) * width + column)
    below = main + PARTS * tail * LANES
    wanted = jnp.where(row >= slab_height, below + (row - slab_height) * width + column, wanted)
    wanted = jnp.where(row < slab_height + MARGIN, wanted, -1)
    in_tail = (row >= MARGIN) & (row < slab_height)
    tail_width = (slab_height - MARGIN) * width
    other = jnp.where(in_tail, wanted + tail * LANES + tail_width, -1)
    for at in range(0, pick.shape[0], LANES):
        source = at + lax.broadcasted_iota(jnp.int32, (LANES, pick.shape[1]), 0)
        taken = (source == wanted) | (source == other)
        pick[at:at + LANES, :] = jnp.where(taken, 1.0, 0.0).astype(jnp.bfloat16)


def kernel(axis, slab_height, width, x_ref, out_ref, slab, below, pick, high, low, partial,
           send_sem, recv_sem, fsend_sem, frecv_sem, own_sem):
    count, dates = slab.shape[1], slab.shape[1] * slab.shape[2]
    blocks = below.shape[0] // PARTS
    groups = width // STEP_RG
    out_rows = slab_height // STEP_AZ
    me = lax.axis_index(axis)
    before = lax.rem(me + count - 1, count)
    barrier = pltpu.get_barrier_semaphore()

    def greet(step, carry):
        pl.semaphore_signal(barrier, inc=1, device_id={axis: lax.rem(me + step, count)}, device_id_type=MESH)
        return carry

    lax.fori_loop(1, count, greet, 0)
    pl.semaphore_wait(barrier, count - 1)

    def slab_copy(step, to, source):
        return pltpu.make_async_remote_copy(
            src_ref=x_ref.at[to],
            dst_ref=slab.at[:, source],
            send_sem=send_sem.at[step],
            recv_sem=recv_sem.at[step],
            device_id={axis: to},
            device_id_type=MESH,
        )

    def below_copy(block):
        return pltpu.make_async_remote_copy(
            src_ref=slab.at[pl.ds(PARTS * block, PARTS)],
            dst_ref=below.at[pl.ds(PARTS * block, PARTS)],
            send_sem=fsend_sem.at[block],
            recv_sem=frecv_sem.at[block],
            device_id={axis: before},
            device_id_type=MESH,
        )

    def start(step, carry):
        slab_copy(step, lax.rem(me + step, count), me).start()
        return carry

    lax.fori_loop(1, count, start, 0)
    own = pltpu.make_async_copy(x_ref.at[me], slab.at[:, me], own_sem)
    own.start()
    fill_pick(pick, blocks, 1, slab_height, width)
    own.wait()

    def arrive(step, carry):
        source = lax.rem(me + count - step, count)
        slab_copy(step, source, source).wait_recv()
        return carry

    lax.fori_loop(1, count, arrive, 0)

    @pl.when(me > 0)
    def _():
        for block in range(blocks):
            below_copy(block).start()

    for part in range(PARTS):
        tiles = [PARTS * block + part for block in range(blocks)] + [PARTS * blocks]
        value = jnp.concatenate([slab[t].reshape(dates, LANES) for t in tiles], axis=1)
        main = blocks * LANES
        mine = jnp.concatenate([pick[0:main, :], pick[main + part * LANES:main + (part + 1) * LANES, :]], axis=0)
        for half, held in zip(split_in_two(value), (high, low)):
            moved = jnp.dot(half, mine, preferred_element_type=jnp.float32)
            held[part * dates:(part + 1) * dates, :] = moved.astype(jnp.bfloat16)

    lane = lax.broadcasted_iota(jnp.int32, (1, LANES), 1)
    row, column = lane // STEP_RG, lane % STEP_RG
    half_dates = dates // 2
    lower = lax.broadcasted_iota(jnp.int32, (half_dates, half_dates), 0)
    upper = lax.broadcasted_iota(jnp.int32, (half_dates, half_dates), 1)
    real_side, diagonal = upper >= lower, upper == lower
    reach = (BOX_RG - 1) // STEP_RG
    short = BOX_RG - reach * STEP_RG

    def packed(group, inside):
        at = slice(group * LANES, (group + 1) * LANES)
        rh, rl = high[0:dates, at], low[0:dates, at]
        ih, il = high[dates:, at], low[dates:, at]
        keep = jnp.where(inside, 1.0, 0.0).astype(jnp.bfloat16)
        rhm, rlm, ihm, ilm = rh * keep, rl * keep, ih * keep, il * keep
        right = jnp.concatenate([rh, rl, rh, ih, il, ih], axis=1)
        left_re = jnp.concatenate([rhm, rhm, rlm, ihm, ihm, ilm], axis=1)
        left_im = jnp.concatenate([ihm, ihm, ilm, -rhm, -rhm, -rlm], axis=1)

        def dot(left, right):
            return lax.dot_general(left, right, CONTRACT_LANES, preferred_element_type=jnp.float32)

        top = dot(left_re[:half_dates], right)
        bottom = dot(left_im[half_dates:], right)
        top_imag = dot(left_im[:half_dates], right[:half_dates])
        bottom_real = dot(left_re[half_dates:], right[half_dates:])
        return (
            jnp.where(real_side, top[:, :half_dates], top_imag),
            top[:, half_dates:],
            bottom[:, :half_dates],
            jnp.where(real_side, bottom_real, bottom[:, half_dates:]),
        )

    def held_partial(group):
        return tuple(partial[group, block] for block in range(4))

    def hold_partial(group, blocks_of):
        for block in range(4):
            partial[group, block] = blocks_of[block]

    def add(one, two):
        return tuple(a + b for a, b in zip(one, two))

    def write(out_row, at, terms):
        total = functools.reduce(add, terms)
        down, across = [], []
        for block in (total[0], total[3]):
            power = jnp.where(diagonal, block, 0.0)
            down.append(lax.rsqrt(jnp.sum(power, axis=1, keepdims=True)))
            across.append(lax.rsqrt(jnp.sum(power, axis=0, keepdims=True)))
        for block in range(4):
            m, n = block // 2, block % 2
            scaled = total[block] * (down[m] * across[n])
            out_ref[out_row, at, m * half_dates:(m + 1) * half_dates, n * half_dates:(n + 1) * half_dates] = (
                scaled.astype(out_ref.dtype))

    def one_row(out_row, carry):
        @pl.when(me < count - 1)
        def _():
            below_copy(out_row).wait_recv()
            at = (blocks + PARTS) * LANES + out_row * LANES
            mine = pick[pl.ds(pl.multiple_of(at, LANES), LANES), :]
            for part in range(PARTS):
                value = below[PARTS * out_row + part].reshape(dates, LANES)
                for half, held in zip(split_in_two(value), (high, low)):
                    moved = jnp.dot(half, mine, preferred_element_type=jnp.float32)
                    here = slice(part * dates, (part + 1) * dates)
                    held[here, :] = held[here, :] + moved.astype(jnp.bfloat16)

        first = out_row * STEP_AZ
        in_rows = (row >= first) & (row < first + BOX_AZ)
        for group in range(groups):
            if group >= reach:
                total = packed(group, in_rows & (column < short))
                write(out_row, group - reach, [held_partial(g) for g in range(group - reach, group)] + [total])
                hold_partial(group, add(total, packed(group, in_rows & (column >= short))))
            else:
                hold_partial(group, packed(group, in_rows))
        for group in range(max(0, groups - reach), groups):
            write(out_row, group, [held_partial(g) for g in range(group, groups)])
        return carry

    lax.fori_loop(0, out_rows, one_row, 0)

    def sent(step, carry):
        slab_copy(step, lax.rem(me + step, count), me).wait_send()
        return carry

    lax.fori_loop(1, count, sent, 0)

    @pl.when(me > 0)
    def _():
        for block in range(blocks):
            below_copy(block).wait_send()


def on_device(slc):
    axis = "date"
    count = lax.axis_size(axis)
    parts, own_dates, height, width = slc.shape
    slab_height = height // count
    out_rows = slab_height // STEP_AZ
    main, tail = MARGIN * width, (slab_height - MARGIN) * width
    blocks = main // LANES
    groups = width // STEP_RG
    dates = count * own_dates
    assert main % LANES == 0 and parts * tail <= LANES and blocks == out_rows
    slabs = slc.reshape(parts, own_dates, count, slab_height * width)
    first = slabs[..., :main].reshape(parts, own_dates, count, blocks, LANES)
    first = first.transpose(2, 3, 0, 1, 4).reshape(count, blocks * parts, own_dates, LANES)
    last = slabs[..., main:].transpose(2, 1, 0, 3).reshape(count, 1, own_dates, parts * tail)
    last = jnp.pad(last, ((0, 0),) * 3 + ((0, LANES - parts * tail),))
    messages = jnp.concatenate([first, last], axis=1)
    wide = groups * LANES
    return pl.pallas_call(
        functools.partial(kernel, axis, slab_height, width),
        out_shape=jax.ShapeDtypeStruct((out_rows, groups, dates, dates), jnp.bfloat16),
        in_specs=[pl.BlockSpec(memory_space=pltpu.VMEM)],
        out_specs=pl.BlockSpec(memory_space=pltpu.VMEM),
        scratch_shapes=[
            pltpu.VMEM((parts * blocks + 1, count, own_dates, LANES), jnp.float32),
            pltpu.VMEM((parts * blocks, count, own_dates, LANES), jnp.float32),
            pltpu.VMEM(((2 * blocks + parts) * LANES, wide), jnp.bfloat16),
            pltpu.VMEM((parts * dates, wide), jnp.bfloat16),
            pltpu.VMEM((parts * dates, wide), jnp.bfloat16),
            pltpu.VMEM((groups, 4, dates // 2, dates // 2), jnp.float32),
            pltpu.SemaphoreType.DMA((count,)),
            pltpu.SemaphoreType.DMA((count,)),
            pltpu.SemaphoreType.DMA((blocks,)),
            pltpu.SemaphoreType.DMA((blocks,)),
            pltpu.SemaphoreType.DMA,
        ],
        compiler_params=pltpu.CompilerParams(
            collective_id=0, has_side_effects=True, vmem_limit_bytes=48 * 1024 * 1024
        ),
    )(messages)


def solution(mesh):
    in_specs = (P(None, "date", "frames", None),)
    out_specs = P(("frames", "date"), None, None, None)
    return jax.shard_map(
        on_device, mesh=mesh, in_specs=in_specs, out_specs=out_specs, check_vma=False
    )
```

```python
import functools

import jax
import jax.numpy as jnp
from jax import lax
from jax.experimental import pallas as pl
from jax.experimental.pallas import tpu as pltpu
from jax.sharding import PartitionSpec as P

BOX_AZ = 11
BOX_RG = 23
STEP_AZ = 3
STEP_RG = 6
MARGIN = 8
LANES = 128
PARTS = 2
MESH = pl.DeviceIdType.MESH
CONTRACT_LANES = (((1,), (1,)), ((), ()))


def round_up(value, multiple):
    return -(-value // multiple) * multiple


def split_in_two(value):
    big = value.astype(jnp.bfloat16)
    return big, (value - big.astype(jnp.float32)).astype(jnp.bfloat16)


def fill_pick(pick, blocks, tail, slab_height, width):
    target = lax.broadcasted_iota(jnp.int32, (1, pick.shape[1]), 1)
    within = target % LANES
    row, column = within // STEP_RG, target // LANES * STEP_RG + within % STEP_RG
    main = blocks * LANES
    wanted = jnp.where(row < MARGIN, row * width + column, main + (row - MARGIN) * width + column)
    below = main + PARTS * tail * LANES
    wanted = jnp.where(row >= slab_height, below + (row - slab_height) * width + column, wanted)
    wanted = jnp.where(row < slab_height + MARGIN, wanted, -1)
    in_tail = (row >= MARGIN) & (row < slab_height)
    tail_width = (slab_height - MARGIN) * width
    other = jnp.where(in_tail, wanted + tail * LANES + tail_width, -1)
    for at in range(0, pick.shape[0], LANES):
        source = at + lax.broadcasted_iota(jnp.int32, (LANES, pick.shape[1]), 0)
        taken = (source == wanted) | (source == other)
        pick[at:at + LANES, :] = jnp.where(taken, 1.0, 0.0).astype(jnp.bfloat16)


def kernel(axis, slab_height, width, x_ref, out_ref, slab, below, pick, high, low, partial,
           send_sem, recv_sem, fsend_sem, frecv_sem, own_sem):
    count, dates = slab.shape[1], slab.shape[1] * slab.shape[2]
    blocks = below.shape[0] // PARTS
    groups = width // STEP_RG
    out_rows = slab_height // STEP_AZ
    me = lax.axis_index(axis)
    before = lax.rem(me + count - 1, count)
    barrier = pltpu.get_barrier_semaphore()

    def greet(step, carry):
        pl.semaphore_signal(barrier, inc=1, device_id={axis: lax.rem(me + step, count)}, device_id_type=MESH)
        return carry

    lax.fori_loop(1, count, greet, 0)
    pl.semaphore_wait(barrier, count - 1)

    def slab_copy(step, to, source):
        return pltpu.make_async_remote_copy(
            src_ref=x_ref.at[to],
            dst_ref=slab.at[:, source],
            send_sem=send_sem.at[step],
            recv_sem=recv_sem.at[step],
            device_id={axis: to},
            device_id_type=MESH,
        )

    def below_copy(block):
        return pltpu.make_async_remote_copy(
            src_ref=slab.at[pl.ds(PARTS * block, PARTS)],
            dst_ref=below.at[pl.ds(PARTS * block, PARTS)],
            send_sem=fsend_sem.at[block],
            recv_sem=frecv_sem.at[block],
            device_id={axis: before},
            device_id_type=MESH,
        )

    def start(step, carry):
        slab_copy(step, lax.rem(me + step, count), me).start()
        return carry

    lax.fori_loop(1, count, start, 0)
    own = pltpu.make_async_copy(x_ref.at[me], slab.at[:, me], own_sem)
    own.start()
    fill_pick(pick, blocks, 1, slab_height, width)
    own.wait()

    def arrive(step, carry):
        source = lax.rem(me + count - step, count)
        slab_copy(step, source, source).wait_recv()
        return carry

    lax.fori_loop(1, count, arrive, 0)

    @pl.when(me > 0)
    def _():
        for block in range(blocks):
            below_copy(block).start()

    for part in range(PARTS):
        tiles = [PARTS * block + part for block in range(blocks)] + [PARTS * blocks]
        value = jnp.concatenate([slab[t].reshape(dates, LANES) for t in tiles], axis=1)
        main = blocks * LANES
        mine = jnp.concatenate([pick[0:main, :], pick[main + part * LANES:main + (part + 1) * LANES, :]], axis=0)
        for half, held in zip(split_in_two(value), (high, low)):
            moved = jnp.dot(half, mine, preferred_element_type=jnp.float32)
            held[part * dates:(part + 1) * dates, :] = moved.astype(jnp.bfloat16)

    lane = lax.broadcasted_iota(jnp.int32, (1, LANES), 1)
    row, column = lane // STEP_RG, lane % STEP_RG
    half_dates = dates // 2
    lower = lax.broadcasted_iota(jnp.int32, (half_dates, half_dates), 0)
    upper = lax.broadcasted_iota(jnp.int32, (half_dates, half_dates), 1)
    real_side, diagonal = upper >= lower, upper == lower
    reach = (BOX_RG - 1) // STEP_RG
    short = BOX_RG - reach * STEP_RG

    def packed(group, insides):
        at = slice(group * LANES, (group + 1) * LANES)
        rh, rl = high[0:dates, at], low[0:dates, at]
        ih, il = high[dates:, at], low[dates:, at]
        right = jnp.concatenate([rh, rl, rh, ih, il, ih], axis=1)
        full, top_imag, bottom_real = [], [], []
        for inside in insides:
            keep = jnp.where(inside, 1.0, 0.0).astype(jnp.bfloat16)
            rhm, rlm, ihm, ilm = rh * keep, rl * keep, ih * keep, il * keep
            left_re = jnp.concatenate([rhm, rhm, rlm, ihm, ihm, ilm], axis=1)
            left_im = jnp.concatenate([ihm, ihm, ilm, -rhm, -rhm, -rlm], axis=1)
            full += [left_re[:half_dates], left_im[half_dates:]]
            top_imag.append(left_im[:half_dates])
            bottom_real.append(left_re[half_dates:])

        def dot(lefts, right):
            left = jnp.concatenate(lefts, axis=0)
            return lax.dot_general(left, right, CONTRACT_LANES, preferred_element_type=jnp.float32)

        full = dot(full, right)
        top_imag = dot(top_imag, right[:half_dates])
        bottom_real = dot(bottom_real, right[half_dates:])
        blocks_of = []
        for index in range(len(insides)):
            here = slice(index * half_dates, (index + 1) * half_dates)
            top = full[2 * index * half_dates:(2 * index + 1) * half_dates]
            bottom = full[(2 * index + 1) * half_dates:(2 * index + 2) * half_dates]
            blocks_of.append((
                jnp.where(real_side, top[:, :half_dates], top_imag[here]),
                top[:, half_dates:],
                bottom[:, :half_dates],
                jnp.where(real_side, bottom_real[here], bottom[:, half_dates:]),
            ))
        return blocks_of

    def held_partial(group):
        return tuple(partial[group, block] for block in range(4))

    def hold_partial(group, blocks_of):
        for block in range(4):
            partial[group, block] = blocks_of[block]

    def add(one, two):
        return tuple(a + b for a, b in zip(one, two))

    def write(out_row, at, terms):
        total = functools.reduce(add, terms)
        down, across = [], []
        for block in (total[0], total[3]):
            power = jnp.where(diagonal, block, 0.0)
            down.append(lax.rsqrt(jnp.sum(power, axis=1, keepdims=True)))
            across.append(lax.rsqrt(jnp.sum(power, axis=0, keepdims=True)))
        for block in range(4):
            m, n = block // 2, block % 2
            scaled = total[block] * (down[m] * across[n])
            out_ref[out_row, at, m * half_dates:(m + 1) * half_dates, n * half_dates:(n + 1) * half_dates] = (
                scaled.astype(out_ref.dtype))

    def one_row(out_row, carry):
        @pl.when(me < count - 1)
        def _():
            below_copy(out_row).wait_recv()
            at = (blocks + PARTS) * LANES + out_row * LANES
            mine = pick[pl.ds(pl.multiple_of(at, LANES), LANES), :]
            for part in range(PARTS):
                value = below[PARTS * out_row + part].reshape(dates, LANES)
                for half, held in zip(split_in_two(value), (high, low)):
                    moved = jnp.dot(half, mine, preferred_element_type=jnp.float32)
                    here = slice(part * dates, (part + 1) * dates)
                    held[here, :] = held[here, :] + moved.astype(jnp.bfloat16)

        first = out_row * STEP_AZ
        in_rows = (row >= first) & (row < first + BOX_AZ)
        for group in range(groups):
            if group >= reach:
                total, rest = packed(group, [in_rows & (column < short), in_rows & (column >= short)])
                write(out_row, group - reach, [held_partial(g) for g in range(group - reach, group)] + [total])
                hold_partial(group, add(total, rest))
            else:
                hold_partial(group, packed(group, [in_rows])[0])
        for group in range(max(0, groups - reach), groups):
            write(out_row, group, [held_partial(g) for g in range(group, groups)])
        return carry

    lax.fori_loop(0, out_rows, one_row, 0)

    def sent(step, carry):
        slab_copy(step, lax.rem(me + step, count), me).wait_send()
        return carry

    lax.fori_loop(1, count, sent, 0)

    @pl.when(me > 0)
    def _():
        for block in range(blocks):
            below_copy(block).wait_send()


def on_device(slc):
    axis = "date"
    count = lax.axis_size(axis)
    parts, own_dates, height, width = slc.shape
    slab_height = height // count
    out_rows = slab_height // STEP_AZ
    main, tail = MARGIN * width, (slab_height - MARGIN) * width
    blocks = main // LANES
    groups = width // STEP_RG
    dates = count * own_dates
    assert main % LANES == 0 and parts * tail <= LANES and blocks == out_rows
    slabs = slc.reshape(parts, own_dates, count, slab_height * width)
    first = slabs[..., :main].reshape(parts, own_dates, count, blocks, LANES)
    first = first.transpose(2, 3, 0, 1, 4).reshape(count, blocks * parts, own_dates, LANES)
    last = slabs[..., main:].transpose(2, 1, 0, 3).reshape(count, 1, own_dates, parts * tail)
    last = jnp.pad(last, ((0, 0),) * 3 + ((0, LANES - parts * tail),))
    messages = jnp.concatenate([first, last], axis=1)
    wide = groups * LANES
    return pl.pallas_call(
        functools.partial(kernel, axis, slab_height, width),
        out_shape=jax.ShapeDtypeStruct((out_rows, groups, dates, dates), jnp.bfloat16),
        in_specs=[pl.BlockSpec(memory_space=pltpu.VMEM)],
        out_specs=pl.BlockSpec(memory_space=pltpu.VMEM),
        scratch_shapes=[
            pltpu.VMEM((parts * blocks + 1, count, own_dates, LANES), jnp.float32),
            pltpu.VMEM((parts * blocks, count, own_dates, LANES), jnp.float32),
            pltpu.VMEM(((2 * blocks + parts) * LANES, wide), jnp.bfloat16),
            pltpu.VMEM((parts * dates, wide), jnp.bfloat16),
            pltpu.VMEM((parts * dates, wide), jnp.bfloat16),
            pltpu.VMEM((groups, 4, dates // 2, dates // 2), jnp.float32),
            pltpu.SemaphoreType.DMA((count,)),
            pltpu.SemaphoreType.DMA((count,)),
            pltpu.SemaphoreType.DMA((blocks,)),
            pltpu.SemaphoreType.DMA((blocks,)),
            pltpu.SemaphoreType.DMA,
        ],
        compiler_params=pltpu.CompilerParams(
            collective_id=0, has_side_effects=True, vmem_limit_bytes=48 * 1024 * 1024
        ),
    )(messages)


def solution(mesh):
    in_specs = (P(None, "date", "frames", None),)
    out_specs = P(("frames", "date"), None, None, None)
    return jax.shard_map(
        on_device, mesh=mesh, in_specs=in_specs, out_specs=out_specs, check_vma=False
    )
```
